256 devices in a mesh: grp: 8 (over x, core), row: 32 (over y, z).
Axes of the slice: x: 4, y: 4, z: 8, core: 2. Of those that a mesh axis runs over, the one named last changes fastest.
Arguments:
- states: bfloat16 [524288, 256], P(('grp', 'row')), may hold values from -6 to 6
- position: bfloat16 [524288], P(('grp', 'row')), may hold values from 0 to 3
- obs_row: int32 [4096, 128], P(('grp', 'row')), may hold values from 0 to 127
- obs_weight: bfloat16 [524288, 256], P(('grp', 'row')), may hold values from -4 to 4
- send_block: int32 [8192, 1], P(('grp', 'row')), may hold values from 0 to 15
- loc_table: int32 [4096, 16], P(('grp', 'row')), may hold values from 0 to 51, as said below
- loc_count: int32 [4096], P(('grp', 'row')), may hold values from 1 to 16
- theta: float32 [64, 256], replicated, may hold values from -6 to 6
Outputs:
- analysis: bfloat16 [524288, 256], P(('grp', 'row'))
- theta_new: float32 [64, 256], P(None, 'row')
The draws below stay inside these ranges and needn't reach their ends.
Inputs may be any that keep to these rules, and one draw needn't show every extreme that they name: `loc_table`: each block's list holds 16 different table entries; its first is the block itself, entry 2 plus the block's index on its device.
All inputs are finite; a program needn't handle non-finite values.
Results may differ from the reference program's by a relative error of at most 0.01.
Values may be sent and summed in bfloat16 or wider, within the bound.
A program may use at most 128 MiB of HBM per device.

```python
import math
import jax
import jax.numpy as jnp
from jax import lax

MEMBERS = 256
BLK = 128
OBS_BLK = 128
LOC = 16
CAP = 1
HB = 2
PARAMS = 64
NB_DEV = 16
NBLK = 4096
NROW = 524288
NOBS = 524288
TABLE = 52
N_GRP = 8
N_ROW = 32
DEVICES = 256


def draw_loc_table(key, part):
    column = jnp.arange(TABLE, dtype=jnp.int32)
    scores = jax.random.randint(key, (NBLK, TABLE), 0, 1 << 20, dtype=jnp.int32) * TABLE + column[None, :]
    own = HB + jnp.arange(NBLK, dtype=jnp.int32) % NB_DEV
    scores = jnp.where(column[None, :] == own[:, None], -1, scores)
    order = jnp.argsort(scores, axis=1)
    return order[:, :LOC].astype(jnp.int32)


def touch_ends(values, own_key, least, largest):
    shape = values.shape
    spot = [jax.random.randint(jax.random.fold_in(own_key, axis), (), 0, shape[axis]) for axis in range(len(shape))]
    values = values.at[tuple(spot)].set(least)
    longest = shape.index(max(shape))
    spot[longest] = (spot[longest] + 1) % shape[longest]
    return values.at[tuple(spot)].set(largest)


def level_of(rng, shape, shards, low, largest):
    gain, own = 1.0, jax.random.fold_in(rng, 6)
    for axis_at, shards_of in shards:
        draws = jnp.exp(jax.random.uniform(jax.random.fold_in(own, axis_at), (shards_of,), jnp.float32, low / len(shards), largest / len(shards)))
        gain = gain * jnp.repeat(draws, shape[axis_at] // shards_of).reshape([-1 if axis == axis_at else 1 for axis in range(len(shape))])
    return gain


def centred(own_key, extent, spread, limit, split=(), kind=jnp.bfloat16):
    level = level_of(own_key, extent, split, -0.22, 0.18) if split else 1.0
    entries = jax.random.normal(own_key, extent, jnp.float32) * spread * level
    return jnp.minimum(jnp.maximum(entries, -limit), limit).astype(kind)


def setup_inputs(seed: int = 0) -> dict:
    streams_of = jax.random.split(jax.random.key(seed), 9)
    states = centred(streams_of[0], (NROW, MEMBERS), 1.0, 6.0, ((0, 256),))
    position = jnp.clip(3.0 * jax.random.uniform(streams_of[1], (NROW,), jnp.float32) ** level_of(streams_of[1], (NROW,), ((0, 256),), -0.2, 0.2), 0.0, 3.0).astype(jnp.bfloat16)
    obs_row = touch_ends(jax.random.randint(streams_of[2], (NBLK, OBS_BLK), 0, BLK), jax.random.fold_in(streams_of[2], 1), 0, BLK - 1).astype(jnp.int32)
    obs_weight = centred(streams_of[3], (NOBS, MEMBERS), 0.5, 4.0, ((0, 256),))
    send_block = touch_ends(jax.random.randint(streams_of[4], (DEVICES * N_ROW, CAP), 0, NB_DEV), jax.random.fold_in(streams_of[4], 1), 0, NB_DEV - 1).astype(jnp.int32)
    loc_table = draw_loc_table(jax.random.fold_in(streams_of[8], 71), 0)
    loc_count = touch_ends(jax.random.randint(streams_of[6], (NBLK,), 1, LOC + 1), jax.random.fold_in(streams_of[6], 1), 1, LOC).astype(jnp.int32)
    theta = centred(streams_of[7], (PARAMS, MEMBERS), 1.0, 6.0, (), jnp.float32)
    return dict(states=states, position=position, obs_row=obs_row, obs_weight=obs_weight, send_block=send_block, loc_table=loc_table, loc_count=loc_count, theta=theta)


def build_table(send_block):
    dev = jnp.arange(DEVICES, dtype=jnp.int32)
    grp_of = dev // N_ROW
    row_of = dev % N_ROW
    left_dev = (grp_of - 1) % N_GRP * N_ROW + row_of
    right_dev = (grp_of + 1) % N_GRP * N_ROW + row_of
    left = left_dev[:, None] * NB_DEV + (NB_DEV - HB + jnp.arange(HB, dtype=jnp.int32))[None, :]
    own = dev[:, None] * NB_DEV + jnp.arange(NB_DEV, dtype=jnp.int32)[None, :]
    right = right_dev[:, None] * NB_DEV + jnp.arange(HB, dtype=jnp.int32)[None, :]
    slot = jnp.arange(N_ROW * CAP, dtype=jnp.int32)
    sender = grp_of[:, None] * N_ROW + (slot // CAP)[None, :]
    local = send_block[sender * N_ROW + row_of[:, None], (slot % CAP)[None, :]]
    recv = sender * NB_DEV + local
    return jnp.concatenate([left, own, right, recv], axis=1).astype(jnp.int32)

def reference(states, position, obs_row, obs_weight, send_block, loc_table, loc_count, theta):
    whole = states.astype(jnp.float32)
    anomaly = (whole - lax.optimization_barrier(jnp.mean(whole, axis=1, keepdims=True))).astype(jnp.bfloat16)
    blocks = anomaly.reshape(NBLK, BLK, MEMBERS)
    places = position.reshape(NBLK, BLK)
    predicted = jnp.take_along_axis(blocks, obs_row[:, :, None], axis=1)
    obs_place = jnp.take_along_axis(places, obs_row, axis=1)
    weights = obs_weight.reshape(NBLK, OBS_BLK, MEMBERS)
    table = build_table(send_block)
    owner = jnp.arange(NBLK, dtype=jnp.int32) // NB_DEV
    source = jnp.take_along_axis(table[owner], loc_table, axis=1)

    def one_block(item):
        xb, pb, ids, cnt = item
        tiles = predicted[ids].astype(jnp.float32)
        wts = weights[ids].astype(jnp.float32)
        pts = obs_place[ids].astype(jnp.float32)
        scores = jnp.einsum('im,ljm->lij', xb.astype(jnp.float32), tiles)
        gap = pb.astype(jnp.float32)[None, :, None] - pts[:, None, :]
        taper = 1.0 / (1.0 + gap * gap)
        live = jnp.arange(LOC, dtype=jnp.int32) < cnt
        mix = jnp.where(live[:, None, None], taper * scores / (MEMBERS - 1), 0.0).astype(jnp.bfloat16)
        return jnp.einsum('lij,ljm->im', mix.astype(jnp.float32), wts)
    gains = lax.map(one_block, (blocks, places, source, loc_count))
    analysis = (whole + gains.reshape(NROW, MEMBERS)).astype(jnp.bfloat16)
    pred_rows = predicted.reshape(NOBS, MEMBERS)
    cross = jnp.dot(pred_rows.T, obs_weight, preferred_element_type=jnp.float32)
    theta_anom = theta - lax.optimization_barrier(jnp.mean(theta, axis=1, keepdims=True))
    update = jnp.dot(theta_anom, cross, precision=lax.Precision.HIGHEST)
    theta_new = theta + update / math.sqrt(MEMBERS * NOBS)
    return (analysis, theta_new)
```

```python
import functools
import math

import jax
import jax.numpy as jnp
from jax import lax
from jax.experimental import pallas as pl
from jax.experimental.pallas import tpu as pltpu
from jax.sharding import PartitionSpec as P

MESH = pl.DeviceIdType.MESH
NG, NY, NZ = 8, 4, 8
NR = NY * NZ
NB, BLK, MEM = 16, 128, 256
HALO = 2
LOCAL = NB + 2 * HALO
LISTS = 16
PARAMS = 64
COLS = MEM // NR
WIDE = MEM + 128
SENT = 128
ROOT = math.sqrt(MEM - 1.0)
FAR = 1.5e19
F32, BF16 = jnp.float32, jnp.bfloat16
NT = (((1,), (1,)), ((), ()))
TN = (((0,), (0,)), ((), ()))


def mm(a, b, dims=None):
    if dims is None:
        return jnp.dot(a, b, preferred_element_type=F32)
    return lax.dot_general(a, b, dims, preferred_element_type=F32)


def shift_of(i):
    k = i // NY
    odd = k % 2
    return i % NY, odd * ((k + 1) // 2) + (1 - odd) * ((NZ - k // 2) % NZ)


def row_at(r, i, sign):
    dy, dz = shift_of(i)
    y, z = r // NZ, r % NZ
    return (y + sign * dy + NY) % NY * NZ + (z + sign * dz + NZ) % NZ


def iota(shape, dim):
    return lax.broadcasted_iota(jnp.int32, shape, dim)


def kernel(
    states, wts, pos, obs, loc, theta, send_block, count,
    out, theta_out,
    lx, lw, lq, comp, compq, outbox, outq, inbox, inq, acc, pb, member, qmask,
    cross_a, cross_b, st1, rv1, st2, rv2, s2, rv3,
    s_data, r_data, s_pos, r_pos, s_halo, r_halo, s_one, r_one, s_two, r_two, s_three, r_three,
):
    g, r = lax.axis_index("grp"), lax.axis_index("row")

    def row_peer(i, sign=1):
        return (g, row_at(r, i, sign))

    def grp_peer(d):
        return ((g + d) % NG, r)

    barrier = pltpu.get_barrier_semaphore()

    @pl.loop(1, NR)
    def _(i):
        pl.semaphore_signal(barrier, inc=1, device_id=row_peer(i), device_id_type=MESH)

    @pl.loop(1, NG)
    def _(d):
        pl.semaphore_signal(barrier, inc=1, device_id=grp_peer(d), device_id_type=MESH)

    below = (iota((BLK, BLK), 0) < iota((BLK, BLK), 1)).astype(BF16)
    same = iota((BLK, BLK), 0) == iota((BLK, BLK), 1)
    ones = jnp.ones((BLK, BLK), BF16)

    @pl.loop(0, NB)
    def _(b):
        whole = states[b].astype(F32)
        anomaly = (whole - jnp.mean(whole, axis=1, keepdims=True)).astype(BF16)
        lx[HALO + b] = anomaly
        picks = (iota((BLK, BLK), 0) == obs[b]).astype(BF16)
        summed = mm(picks, wts[b]).astype(BF16)
        lw[HALO + b] = summed
        place = pos[b]
        lq[HALO + b] = place
        spread = jnp.where(same, jnp.broadcast_to(place, (BLK, BLK)), 0.0).astype(BF16)
        pb[b] = mm(spread, ones) * ROOT
        comp[b, 0:SENT] = anomaly
        comp[b, SENT : 2 * SENT] = summed
        compq[b] = place

    pl.semaphore_wait(barrier, NR - 1 + NG - 1)

    def data_copy(i, sign=1):
        return pltpu.make_async_remote_copy(
            outbox.at[i], inbox.at[i], s_data.at[i], r_data.at[i],
            device_id=row_peer(i, sign), device_id_type=MESH)

    def pos_copy(i, sign=1):
        return pltpu.make_async_remote_copy(
            outq.at[i], inq.at[i], s_pos.at[i], r_pos.at[i],
            device_id=row_peer(i, sign), device_id_type=MESH)

    @pl.loop(1, NR)
    def _(i):
        b = send_block[row_at(r, i, 1), 0]
        outq[i] = compq[b]
        outbox[i] = comp[b]
        pos_copy(i).start()
        data_copy(i).start()

    mine = send_block[r, 0]
    inq[0] = compq[mine]
    inbox[0] = comp[mine]

    def halo_copies():
        found = []
        for side, (first, last, step) in enumerate(((NB, 0, 1), (HALO, LOCAL - HALO, NG - 1))):
            for part, table in enumerate((lx, lw, lq)):
                at = 3 * side + part
                found.append(pltpu.make_async_remote_copy(
                    table.at[pl.ds(first, HALO)], table.at[pl.ds(last, HALO)], s_halo.at[at], r_halo.at[at],
                    device_id=grp_peer(step), device_id_type=MESH))
        return found

    for copy in halo_copies():
        copy.start()

    at_block = iota((NB, 128), 0)
    counts = jnp.zeros((NB, 128), jnp.int32)
    for k in range(NB):
        counts = jnp.where(at_block == k, count[k], counts)
    entry = iota((NB, 128), 1)
    found = jnp.zeros((NB, 128), F32)
    for l in range(LISTS):
        hit = (loc[:, l : l + 1] == entry) & (counts > l)
        found = jnp.where(hit, 1.0, found)
    member[...] = found.astype(BF16)

    cross_a[...] = jnp.zeros_like(cross_a)
    cross_b[...] = jnp.zeros_like(cross_b)

    @pl.loop(0, NB)
    def _(b):
        part = mm(lw[HALO + b], lx[HALO + b], TN)
        cross_a[...] += part[:, :128]
        cross_b[...] += part[:, 128:]
        acc[b] = jnp.zeros((BLK, MEM), F32)

    for d in range(NG):
        st1[d, :, 0:128] = cross_a[pl.ds(d, NR, stride=COLS), :]
        st1[d, :, 128:MEM] = cross_b[pl.ds(d, NR, stride=COLS), :]
        st1[d, :, MEM:WIDE] = jnp.zeros((NR, WIDE - MEM), F32)

    def copy_one(d):
        return pltpu.make_async_remote_copy(
            st1.at[(g + d) % NG], rv1.at[d], s_one.at[d], r_one.at[d], device_id=grp_peer(d), device_id_type=MESH)

    def copy_two(i, sign=1):
        return pltpu.make_async_remote_copy(
            st2.at[row_at(r, i, 1)], rv2.at[i], s_two.at[i], r_two.at[i], device_id=row_peer(i, sign), device_id_type=MESH)

    def copy_three(d):
        return pltpu.make_async_remote_copy(
            s2, rv3.at[d], s_three.at[d], r_three.at[d], device_id=grp_peer(d), device_id_type=MESH)

    @pl.loop(1, NG)
    def _(d):
        copy_one(d).start()

    def masked_place(t, place):
        column = (iota((128, 128), 0) == t).astype(BF16)
        return jnp.where(mm(member[...], column) > 0.5, place * ROOT, FAR)

    def meet(tiles, weights, width, chunk=4):
        for c in range(0, NB, chunk):
            rows = chunk * BLK
            xb = lx[HALO + c : HALO + c + chunk].reshape(rows, MEM)
            score = mm(xb, tiles, NT)
            at_row = jnp.concatenate([pb[c : c + chunk]] * (width // 128), axis=2)
            gap = at_row - qmask[c : c + chunk, :, 0:width]
            den = (gap * gap + (MEM - 1.0)).reshape(rows, width)
            inv = pl.reciprocal(den, approx=True)
            inv = inv * (2.0 - den * inv)
            mix = (score * inv).astype(BF16)
            acc[c : c + chunk] += mm(mix, weights).reshape(chunk, BLK, MEM)

    def put_mask(parts):
        whole = jnp.concatenate(parts, axis=1)
        for k in range(NB):
            qmask[k, :, 0 : whole.shape[1]] = whole[k : k + 1]

    @pl.loop(0, LOCAL // 2)
    def _(it):
        @pl.when(it == NB // 2)
        def _():
            for copy in halo_copies():
                copy.wait()

        p = (it + 1) % (LOCAL // 2)
        put_mask([masked_place(2 * p + e, lq[2 * p + e]) for e in range(2)])
        tiles = lx[pl.ds(2 * p, 2)].reshape(2 * BLK, MEM)
        weights = lw[pl.ds(2 * p, 2)].reshape(2 * BLK, MEM)
        meet(tiles, weights, 2 * BLK)

    @pl.loop(1, NG)
    def _(d):
        copy_one(d).wait()

    s1 = st1[g]
    for d in range(1, NG):
        s1 = s1 + rv1[d]
    for k in range(NR):
        st2[k] = s1[k : k + 1]

    @pl.loop(1, NR)
    def _(i):
        copy_two(i).start()

    rv2[0] = st2[r]

    def two_to_three():
        @pl.loop(1, NR)
        def _(i):
            copy_two(i, -1).wait()

        total = rv2[0]
        for i in range(1, NR):
            total = total + rv2[i]
        s2[...] = total

        @pl.loop(1, NG)
        def _(d):
            copy_three(d).start()

        rv3[0] = total

    def finish_theta():
        @pl.loop(1, NG)
        def _(d):
            copy_three(d).wait()

        found = jnp.zeros((COLS, MEM), F32)
        spot = iota((COLS, MEM), 0)
        for d in range(NG):
            found = jnp.where(spot == (g - d + NG) % NG, rv3[d, :, 0:MEM], found)
        mean = jnp.mean(theta[...], axis=1, keepdims=True)
        update = lax.dot_general(theta[...] - mean, found, NT, precision=lax.Precision.HIGHEST, preferred_element_type=F32)
        chosen = (iota((COLS, MEM), 1) == COLS * r + iota((COLS, MEM), 0)).astype(F32)
        old = lax.dot_general(theta[...], chosen, NT, precision=lax.Precision.HIGHEST, preferred_element_type=F32)
        theta_out[...] = old + update / math.sqrt(MEM * NB * BLK * NG * NR)

    GROUP = 4

    @pl.loop(0, NR // GROUP)
    def _(it):
        @pl.when(it == 5)
        def _():
            two_to_three()

        @pl.when(it == 6)
        def _():
            finish_theta()

        for e in range(GROUP):
            i = GROUP * it + e

            @pl.when(i > 0)
            def _():
                pos_copy(i, -1).wait()
                data_copy(i, -1).wait()

        put_mask([
            masked_place(LOCAL + row_at(r, GROUP * it + e, -1), inq[GROUP * it + e]) for e in range(GROUP)])
        at = pl.ds(GROUP * it, GROUP)
        tiles = inbox[at, 0:SENT, :].reshape(GROUP * SENT, MEM)
        weights = inbox[at, SENT : 2 * SENT, :].reshape(GROUP * SENT, MEM)
        meet(tiles, weights, GROUP * SENT)

    @pl.loop(0, NB)
    def _(b):
        out[b] = (states[b].astype(F32) + acc[b]).astype(BF16)


def per_device(states, position, obs_row, obs_weight, send_block, loc_table, loc_count, theta):
    vmem, smem = pl.BlockSpec(memory_space=pltpu.VMEM), pl.BlockSpec(memory_space=pltpu.SMEM)
    dma = pltpu.SemaphoreType.DMA
    analysis, theta_new = pl.pallas_call(
        kernel,
        out_shape=(
            jax.ShapeDtypeStruct((NB, BLK, MEM), BF16),
            jax.ShapeDtypeStruct((PARAMS, COLS), F32),
        ),
        in_specs=[vmem] * 6 + [smem] * 2,
        out_specs=(vmem, vmem),
        scratch_shapes=[
            pltpu.VMEM((LOCAL, BLK, MEM), BF16),
            pltpu.VMEM((LOCAL, BLK, MEM), BF16),
            pltpu.VMEM((LOCAL, 1, BLK), F32),
            pltpu.VMEM((NB, 2 * SENT, MEM), BF16),
            pltpu.VMEM((NB, 1, BLK), F32),
            pltpu.VMEM((NR, 2 * SENT, MEM), BF16),
            pltpu.VMEM((NR, 1, BLK), F32),
            pltpu.VMEM((NR, 2 * SENT, MEM), BF16),
            pltpu.VMEM((NR, 1, BLK), F32),
            pltpu.VMEM((NB, BLK, MEM), F32),
            pltpu.VMEM((NB, BLK, 128), F32),
            pltpu.VMEM((NB, 128), BF16),
            pltpu.VMEM((NB, 1, 4 * SENT), F32),
            pltpu.VMEM((MEM, 128), F32),
            pltpu.VMEM((MEM, 128), F32),
            pltpu.VMEM((NG, NR, WIDE), F32),
            pltpu.VMEM((NG, NR, WIDE), F32),
            pltpu.VMEM((NR, 1, WIDE), F32),
            pltpu.VMEM((NR, 1, WIDE), F32),
            pltpu.VMEM((1, WIDE), F32),
            pltpu.VMEM((NG, 1, WIDE), F32),
            dma((NR,)), dma((NR,)), dma((NR,)), dma((NR,)), dma((6,)), dma((6,)),
            dma((NG,)), dma((NG,)), dma((NR,)), dma((NR,)), dma((NG,)), dma((NG,)),
        ],
        compiler_params=pltpu.CompilerParams(
            collective_id=0, has_side_effects=True, vmem_limit_bytes=56 * 1024 * 1024
        ),
    )(
        states.reshape(NB, BLK, MEM),
        obs_weight.reshape(NB, BLK, MEM),
        position.astype(F32).reshape(NB, 1, BLK),
        obs_row.reshape(NB, 1, BLK),
        loc_table,
        theta,
        send_block,
        loc_count,
    )
    return analysis.reshape(NB * BLK, MEM), theta_new


def solution(mesh):
    in_specs = (
        P(("grp", "row"), None),
        P(("grp", "row")),
        P(("grp", "row"), None),
        P(("grp", "row"), None),
        P(("grp", "row"), None),
        P(("grp", "row"), None),
        P(("grp", "row")),
        P(),
    )
    out_specs = (P(("grp", "row"), None), P(None, "row"))
    return jax.shard_map(
        per_device, mesh=mesh, in_specs=in_specs, out_specs=out_specs, check_vma=False
    )
```

```python
import functools
import math

import jax
import jax.numpy as jnp
from jax import lax
from jax.experimental import pallas as pl
from jax.experimental.pallas import tpu as pltpu
from jax.sharding import PartitionSpec as P

MESH = pl.DeviceIdType.MESH
NG, NY, NZ = 8, 4, 8
NR = NY * NZ
NB, BLK, MEM = 16, 128, 256
HALO = 2
LOCAL = NB + 2 * HALO
LISTS = 16
PARAMS = 64
COLS = MEM // NR
WIDE = MEM + 128
GROUP = 4
GROUPS = NR // GROUP
AHEAD = 4
SENT = 96
ROOT = math.sqrt(MEM - 1.0)
FAR = 1.5e19
F32, BF16 = jnp.float32, jnp.bfloat16
NT = (((1,), (1,)), ((), ()))
TN = (((0,), (0,)), ((), ()))


def mm(a, b, dims=(((1,), (0,)), ((), ()))):
    return lax.dot_general(a, b, dims, preferred_element_type=F32)


def exact(a, b, dims):
    return lax.dot_general(a, b, dims, precision=lax.Precision.HIGHEST, preferred_element_type=F32)


def iota(shape, dim):
    return lax.broadcasted_iota(jnp.int32, shape, dim)


def row_at(r, i, sign):
    k, dy = i // NY, i % NY
    odd = k % 2
    dz = odd * ((k + 1) // 2) + (1 - odd) * ((NZ - k // 2) % NZ)
    y, z = r // NZ, r % NZ
    return (y + sign * dy + NY) % NY * NZ + (z + sign * dz + NZ) % NZ


def side_by_side(parts, width):
    if width == 128:
        return jnp.concatenate(parts, axis=1)
    lane = iota(parts[0].shape, 1)
    a, b, c, d = parts
    if width == 96:
        b, c, d = pltpu.roll(b, 96, 1), pltpu.roll(c, 64, 1), pltpu.roll(d, 32, 1)
        return jnp.concatenate(
            [jnp.where(lane < 96, a, b), jnp.where(lane < 64, b, c), jnp.where(lane < 32, c, d)], axis=1)
    assert width == 32
    b, c, d = pltpu.roll(b, 32, 1), pltpu.roll(c, 64, 1), pltpu.roll(d, 96, 1)
    return jnp.where(lane < 32, a, jnp.where(lane < 64, b, jnp.where(lane < 96, c, d)))


def observed_rows(obs_row):
    picks = (iota((BLK, BLK), 0) == obs_row).astype(BF16)
    below = (iota((BLK, BLK), 0) < iota((BLK, BLK), 1)).astype(BF16)
    seen = (mm(jnp.ones((8, BLK), BF16), picks, NT) > 0.5).astype(BF16)
    rank = mm(seen, below)
    at = iota((BLK, BLK), 0).astype(F32)
    pack = jnp.where(at == rank[0:1], seen[0:1].astype(F32), 0.0).astype(BF16)
    return picks, seen, pack


def kernel(
    first, sent, whole_job,
    states, wts, pos, obs, loc, theta, send_block, count, acc, theta_out, flag_out,
    lx, lw, lq, comp, compq, outbox, outq, inbox, inq, pb, member, qmask, over,
    cross_a, cross_b, st1, rv1, st2, rv2, s2, rv3,
    s_data, r_data, s_pos, r_pos, s_halo, r_halo, s_one, r_one, s_two, r_two, s_three, r_three,
):
    g, r = lax.axis_index("grp"), lax.axis_index("row")

    def row_peer(i, sign=1):
        return (g, row_at(r, i, sign))

    def grp_peer(d):
        return ((g + d) % NG, r)

    barrier = pltpu.get_barrier_semaphore()

    @pl.loop(1, NR)
    def _(i):
        pl.semaphore_signal(barrier, inc=1, device_id=row_peer(i), device_id_type=MESH)

    if whole_job:

        @pl.loop(1, NG)
        def _(d):
            pl.semaphore_signal(barrier, inc=1, device_id=grp_peer(d), device_id_type=MESH)

        cross_a[...] = jnp.zeros_like(cross_a)
        cross_b[...] = jnp.zeros_like(cross_b)
        over[...] = jnp.zeros_like(over)

    for b in range(NB):
        place = pos[b : b + 1].astype(F32)
        lq[HALO + b] = place

    same = iota((BLK, BLK), 0) == iota((BLK, BLK), 1)
    ones = jnp.ones((BLK, BLK), BF16)
    UNROLL = 4

    @pl.loop(0, NB // UNROLL)
    def _(turn):
        for u in range(UNROLL):
            b = turn * UNROLL + u
            whole = states[b].astype(F32)
            anomaly = (whole - jnp.mean(whole, axis=1, keepdims=True)).astype(BF16)
            lx[HALO + b] = anomaly
            picks, seen, pack = observed_rows(obs[b])
            summed = mm(picks, wts[b]).astype(BF16)
            lw[HALO + b] = summed
            comp[b, 0:sent] = mm(pack, anomaly).astype(BF16)[first : first + sent]
            comp[b, sent : 2 * sent] = mm(pack, summed).astype(BF16)[first : first + sent]
            place = jnp.broadcast_to(lq[HALO + b], (BLK, BLK))
            packed = mm(place[0:16].astype(BF16), pack, NT)[0:1]
            compq[b] = packed if first == 0 else pltpu.roll(packed, BLK - first, 1)
            spread = jnp.where(same, place, 0.0).astype(BF16)
            pb[b] = mm(spread, ones) * ROOT
            acc[b] = jnp.zeros((BLK, MEM), F32)
            if whole_job:
                over[...] += jnp.maximum(mm(seen, ones) - float(sent), 0.0)
                part = mm(summed, anomaly, TN)
                cross_a[...] += part[:, :128]
                cross_b[...] += part[:, 128:]

    if whole_job:
        for d in range(NG):
            st1[d, :, 0:128] = cross_a[pl.ds(d, NR, stride=COLS), :]
            st1[d, :, 128:MEM] = cross_b[pl.ds(d, NR, stride=COLS), :]
            st1[d, :, MEM:WIDE] = jnp.broadcast_to(over[0:1], (NR, WIDE - MEM))

    pl.semaphore_wait(barrier, NR - 1 + (NG - 1 if whole_job else 0))

    def data_copy(i, sign=1):
        return pltpu.make_async_remote_copy(
            outbox.at[i], inbox.at[i], s_data.at[i], r_data.at[i],
            device_id=row_peer(i, sign), device_id_type=MESH)

    def pos_copy(i, sign=1):
        return pltpu.make_async_remote_copy(
            outq.at[i], inq.at[i], s_pos.at[i], r_pos.at[i],
            device_id=row_peer(i, sign), device_id_type=MESH)

    def send(i):
        b = send_block[row_at(r, i, 1)]
        outq[i] = compq[b]
        outbox[i] = comp[b]
        pos_copy(i).start()
        data_copy(i).start()

    def halo_copies():
        found = []
        for side, (start, end, step) in enumerate(((NB, 0, 1), (HALO, LOCAL - HALO, NG - 1))):
            for part, table in enumerate((lx, lw, lq)):
                at = 3 * side + part
                found.append(pltpu.make_async_remote_copy(
                    table.at[pl.ds(start, HALO)], table.at[pl.ds(end, HALO)], s_halo.at[at], r_halo.at[at],
                    device_id=grp_peer(step), device_id_type=MESH))
        return found

    def copy_one(d):
        return pltpu.make_async_remote_copy(
            st1.at[(g + d) % NG], rv1.at[d], s_one.at[d], r_one.at[d], device_id=grp_peer(d), device_id_type=MESH)

    def copy_two(i, sign=1):
        return pltpu.make_async_remote_copy(
            st2.at[row_at(r, i, 1)], rv2.at[i], s_two.at[i], r_two.at[i],
            device_id=row_peer(i, sign), device_id_type=MESH)

    def copy_three(d):
        return pltpu.make_async_remote_copy(
            s2, rv3.at[d], s_three.at[d], r_three.at[d], device_id=grp_peer(d), device_id_type=MESH)

    @pl.loop(1, GROUP * AHEAD)
    def _(i):
        if whole_job:

            @pl.when(i == 2 * GROUP)
            def _():
                @pl.loop(1, NG)
                def _(d):
                    copy_one(d).start()

                for copy in halo_copies():
                    copy.start()

        send(i)

    mine = send_block[r]
    inq[0] = compq[mine]
    inbox[0] = comp[mine]

    at_block = iota((NB, 128), 0)
    counts = jnp.zeros((NB, 128), jnp.int32)
    for k in range(NB):
        counts = jnp.where(at_block == k, count[k], counts)
    entry = iota((NB, 128), 1)
    found = jnp.zeros((NB, 128), F32)
    for l in range(LISTS):
        hit = (loc[:, l : l + 1] == entry) & (counts > l)
        found = jnp.where(hit, 1.0, found)
    member[...] = found.astype(BF16)

    def masked_place(t, place):
        column = (iota((128, 128), 0) == t).astype(BF16)
        return jnp.where(mm(member[...], column) > 0.5, place * ROOT, FAR)

    def meet(tiles, weights, width, chunk=4):
        for c in range(0, NB, chunk):
            rows = chunk * BLK
            xb = lx[HALO + c : HALO + c + chunk].reshape(rows, MEM)
            score = mm(xb, tiles, NT)
            at_row = jnp.concatenate([pb[c : c + chunk]] * (width // 128), axis=2)
            gap = at_row - qmask[c : c + chunk, :, 0:width]
            den = (gap * gap + (MEM - 1.0)).reshape(rows, width)
            inv = pl.reciprocal(den, approx=True)
            inv = inv * (2.0 - den * inv)
            mix = (score * inv).astype(BF16)
            acc[c : c + chunk] += mm(mix, weights).reshape(chunk, BLK, MEM)

    def put_mask(whole):
        for k in range(NB):
            qmask[k, :, 0 : whole.shape[1]] = whole[k : k + 1]

    if whole_job:

        @pl.loop(0, LOCAL // 2)
        def _(it):
            @pl.when(it == NB // 2)
            def _():
                for copy in halo_copies():
                    copy.wait()

            p = (it + 1) % (LOCAL // 2)
            put_mask(jnp.concatenate([masked_place(2 * p + e, lq[2 * p + e]) for e in range(2)], axis=1))
            tiles = lx[pl.ds(2 * p, 2)].reshape(2 * BLK, MEM)
            weights = lw[pl.ds(2 * p, 2)].reshape(2 * BLK, MEM)
            meet(tiles, weights, 2 * BLK)

    def one_to_two():
        @pl.loop(1, NG)
        def _(d):
            copy_one(d).wait()

        s1 = st1[g]
        for d in range(1, NG):
            s1 = s1 + rv1[d]
        for k in range(NR):
            st2[k] = s1[k : k + 1]

        @pl.loop(1, NR)
        def _(i):
            copy_two(i).start()

        rv2[0] = st2[r]

    def two_to_three():
        @pl.loop(1, NR)
        def _(i):
            copy_two(i, -1).wait()

        total = rv2[0]
        for i in range(1, NR):
            total = total + rv2[i]
        s2[...] = total

        @pl.loop(1, NG)
        def _(d):
            copy_three(d).start()

        rv3[0] = total
        flag_out[...] = total[:, MEM:WIDE]

    def finish_theta():
        @pl.loop(1, NG)
        def _(d):
            copy_three(d).wait()

        found = jnp.zeros((COLS, MEM), F32)
        spot = iota((COLS, MEM), 0)
        for d in range(NG):
            found = jnp.where(spot == (g - d + NG) % NG, rv3[d, :, 0:MEM], found)
        mean = jnp.mean(theta[...], axis=1, keepdims=True)
        update = exact(found, theta[...] - mean, NT)
        chosen = (iota((COLS, MEM), 1) == COLS * r + iota((COLS, MEM), 0)).astype(F32)
        old = exact(chosen, theta[...], NT)
        theta_out[...] = old + update / math.sqrt(MEM * NB * BLK * NG * NR)

    @pl.loop(0, GROUPS)
    def _(it):
        if whole_job:

            @pl.when(it == 0)
            def _():
                one_to_two()

            @pl.when(it == GROUPS - 1 - AHEAD)
            def _():
                two_to_three()

            @pl.when(it == GROUPS - 2)
            def _():
                finish_theta()

        @pl.when(it < GROUPS - AHEAD)
        def _():
            @pl.loop(0, GROUP)
            def _(e):
                send(GROUP * (it + AHEAD) + e)

        for e in range(GROUP):
            i = GROUP * it + e

            @pl.when(i > 0)
            def _():
                pos_copy(i, -1).wait()
                data_copy(i, -1).wait()

        put_mask(side_by_side(
            [masked_place(LOCAL + row_at(r, GROUP * it + e, -1), inq[GROUP * it + e]) for e in range(GROUP)], sent))
        at = pl.ds(GROUP * it, GROUP)
        tiles = inbox[at, 0:sent, :].reshape(GROUP * sent, MEM)
        weights = inbox[at, sent : 2 * sent, :].reshape(GROUP * sent, MEM)
        meet(tiles, weights, GROUP * sent)

    if not whole_job:
        theta_out[...] = jnp.zeros_like(theta_out)
        flag_out[...] = jnp.zeros_like(flag_out)


def analyse(args, first, sent, whole_job):
    vmem, smem = pl.BlockSpec(memory_space=pltpu.VMEM), pl.BlockSpec(memory_space=pltpu.SMEM)
    dma = pltpu.SemaphoreType.DMA
    states, position, obs_row, obs_weight, send_block, loc_table, loc_count, theta = args
    return pl.pallas_call(
        functools.partial(kernel, first, sent, whole_job),
        out_shape=(
            jax.ShapeDtypeStruct((NB, BLK, MEM), F32),
            jax.ShapeDtypeStruct((COLS, PARAMS), F32),
            jax.ShapeDtypeStruct((1, 128), F32),
        ),
        in_specs=[vmem] * 6 + [smem] * 2,
        out_specs=(vmem, vmem, vmem),
        scratch_shapes=[
            pltpu.VMEM((LOCAL, BLK, MEM), BF16),
            pltpu.VMEM((LOCAL, BLK, MEM), BF16),
            pltpu.VMEM((LOCAL, 1, BLK), F32),
            pltpu.VMEM((NB, 2 * sent, MEM), BF16),
            pltpu.VMEM((NB, 1, BLK), F32),
            pltpu.VMEM((NR, 2 * sent, MEM), BF16),
            pltpu.VMEM((NR, 1, BLK), F32),
            pltpu.VMEM((NR, 2 * sent, MEM), BF16),
            pltpu.VMEM((NR, 1, BLK), F32),
            pltpu.VMEM((NB, BLK, 128), F32),
            pltpu.VMEM((NB, 128), BF16),
            pltpu.VMEM((NB, 1, GROUP * sent), F32),
            pltpu.VMEM((8, 128), F32),
            pltpu.VMEM((MEM, 128), F32),
            pltpu.VMEM((MEM, 128), F32),
            pltpu.VMEM((NG, NR, WIDE), F32),
            pltpu.VMEM((NG, NR, WIDE), F32),
            pltpu.VMEM((NR, 1, WIDE), F32),
            pltpu.VMEM((NR, 1, WIDE), F32),
            pltpu.VMEM((1, WIDE), F32),
            pltpu.VMEM((NG, 1, WIDE), F32),
            dma((NR,)), dma((NR,)), dma((NR,)), dma((NR,)), dma((6,)), dma((6,)),
            dma((NG,)), dma((NG,)), dma((NR,)), dma((NR,)), dma((NG,)), dma((NG,)),
        ],
        compiler_params=pltpu.CompilerParams(
            collective_id=0 if whole_job else 1, has_side_effects=True, vmem_limit_bytes=48 * 1024 * 1024
        ),
    )(
        states.reshape(NB, BLK, MEM),
        obs_weight.reshape(NB, BLK, MEM),
        position.reshape(NB, BLK),
        obs_row.reshape(NB, 1, BLK),
        loc_table,
        theta,
        send_block.reshape(NR),
        loc_count,
    )


def per_device(*args):
    states = args[0]
    acc, theta_new, flag = analyse(args, 0, SENT, True)

    def add(increment):
        return (states.astype(F32) + increment.reshape(NB * BLK, MEM)).astype(BF16)

    def rest():
        return add(acc + analyse(args, SENT, BLK - SENT, False)[0])

    analysis = add(acc) if SENT == BLK else lax.cond(flag[0, 0] > 0.5, rest, lambda: add(acc))
    return analysis, theta_new.T


def solution(mesh):
    in_specs = (
        P(("grp", "row"), None),
        P(("grp", "row")),
        P(("grp", "row"), None),
        P(("grp", "row"), None),
        P(("grp", "row"), None),
        P(("grp", "row"), None),
        P(("grp", "row")),
        P(),
    )
    out_specs = (P(("grp", "row"), None), P(None, "row"))
    return jax.shard_map(
        per_device, mesh=mesh, in_specs=in_specs, out_specs=out_specs, check_vma=False
    )
```

```python
import functools
import math

import jax
import jax.numpy as jnp
from jax import lax
from jax.experimental import pallas as pl
from jax.experimental.pallas import tpu as pltpu
from jax.sharding import PartitionSpec as P

MESH = pl.DeviceIdType.MESH
NG, NY, NZ = 8, 4, 8
NR = NY * NZ
NB, BLK, MEM = 16, 128, 256
HALO = 2
LOCAL = NB + 2 * HALO
LISTS = 16
PARAMS = 64
COLS = MEM // NR
WIDE = MEM + 128
GROUP = 4
GROUPS = NR // GROUP
FIRST = 2
AHEAD = 5
FLIP = 0
ONE_AT = 1
SUM_AT = 2
END_AT = 6
SENT = 96
ROOT = math.sqrt(MEM - 1.0)
FAR = 1.5e19
F32, BF16 = jnp.float32, jnp.bfloat16
NT = (((1,), (1,)), ((), ()))
TN = (((0,), (0,)), ((), ()))


def mm(a, b, dims=(((1,), (0,)), ((), ()))):
    return lax.dot_general(a, b, dims, preferred_element_type=F32)


def exact(a, b, dims):
    return lax.dot_general(a, b, dims, precision=lax.Precision.HIGHEST, preferred_element_type=F32)


def iota(shape, dim):
    return lax.broadcasted_iota(jnp.int32, shape, dim)


def row_at(r, i, sign):
    div, rem = (int.__floordiv__, int.__mod__) if isinstance(i, int) else (lax.div, lax.rem)
    part, dy, side = div(i, 2 * NY), rem(div(i, 2), NY), rem(i, 2)
    far = div(part + 3, 4)
    hops = far * (FLIP * (4 - 2 * part) + part)
    dz = side * (NZ - hops - (1 - far) * (NZ // 2)) + (1 - side) * hops
    y, z = lax.div(r, NZ), lax.rem(r, NZ)
    return lax.rem(y + sign * dy + NY, NY) * NZ + lax.rem(z + sign * dz + NZ, NZ)


def side_by_side(parts, width):
    if width == 128:
        return jnp.concatenate(parts, axis=1)
    lane = iota(parts[0].shape, 1)
    a, b, c, d = parts
    if width == 96:
        b, c, d = pltpu.roll(b, 96, 1), pltpu.roll(c, 64, 1), pltpu.roll(d, 32, 1)
        return jnp.concatenate(
            [jnp.where(lane < 96, a, b), jnp.where(lane < 64, b, c), jnp.where(lane < 32, c, d)], axis=1)
    assert width == 32
    b, c, d = pltpu.roll(b, 32, 1), pltpu.roll(c, 64, 1), pltpu.roll(d, 96, 1)
    return jnp.where(lane < 32, a, jnp.where(lane < 64, b, jnp.where(lane < 96, c, d)))


def observed_rows(obs_row):
    picks = (iota((BLK, BLK), 0) == obs_row).astype(BF16)
    below = (iota((BLK, BLK), 0) < iota((BLK, BLK), 1)).astype(BF16)
    seen = (mm(jnp.ones((8, BLK), BF16), picks, NT) > 0.5).astype(BF16)
    rank = mm(seen, below)
    at = iota((BLK, BLK), 0).astype(F32)
    pack = jnp.where(at == rank[0:1], seen[0:1].astype(F32), 0.0).astype(BF16)
    return picks, seen, pack


def kernel(
    first, sent, whole_job,
    states_in, wts_in, pos, obs, loc, theta, send_block, count, acc, theta_out, flag_out,
    states, wts, load, places, lx, lw, lq, outbox, outq, inbox, inq, pb, member, qmask, over,
    cross_a, cross_b, st1, rv1, st2, rv2, s2, rv3,
    s_data, r_data, s_pos, r_pos, s_halo, r_halo, s_one, r_one, s_two, r_two, s_three, r_three,
):
    g, r = lax.axis_index("grp"), lax.axis_index("row")

    def row_peer(i, sign=1):
        return (g, row_at(r, i, sign))

    def grp_peer(d):
        return ((g + d) % NG, r)

    barrier = pltpu.get_barrier_semaphore()

    loads = [
        pltpu.make_async_copy(states_in, states, load.at[0]), pltpu.make_async_copy(wts_in, wts, load.at[1])]
    for copy in loads:
        copy.start()
    for i in range(1, NR):
        pl.semaphore_signal(barrier, inc=1, device_id=row_peer(i), device_id_type=MESH)
    if whole_job:
        for d in range(1, NG):
            pl.semaphore_signal(barrier, inc=1, device_id=grp_peer(d), device_id_type=MESH)
        cross_a[...] = jnp.zeros_like(cross_a)
        cross_b[...] = jnp.zeros_like(cross_b)
        over[...] = jnp.zeros_like(over)

    for b in range(NB):
        place = pos[b : b + 1].astype(F32)
        places[b] = place
        lq[HALO + b] = place

    for copy in loads:
        copy.wait()

    def data_copy(i, sign=1):
        return pltpu.make_async_remote_copy(
            outbox.at[i], inbox.at[i], s_data.at[i], r_data.at[i],
            device_id=row_peer(i, sign), device_id_type=MESH)

    def pos_copy(i, sign=1):
        return pltpu.make_async_remote_copy(
            outq.at[i], inq.at[i], s_pos.at[i], r_pos.at[i],
            device_id=row_peer(i, sign), device_id_type=MESH)

    def anomaly_of(b):
        whole = states[b].astype(F32)
        return (whole - jnp.mean(whole, axis=1, keepdims=True)).astype(BF16)

    def build(i):
        b = send_block[row_at(r, i, 1)]
        anomaly, weights = anomaly_of(b), wts[b]
        picks, _, pack = observed_rows(obs[b])
        summed = mm(picks, weights).astype(BF16)
        outbox[i, 0:sent] = mm(pack, anomaly).astype(BF16)[first : first + sent]
        outbox[i, sent : 2 * sent] = mm(pack, summed).astype(BF16)[first : first + sent]
        place = jnp.broadcast_to(places[b], (16, BLK)).astype(BF16)
        packed = mm(place, pack, NT)[0:1]
        outq[i] = packed if first == 0 else pltpu.roll(packed, BLK - first, 1)

    def send(i):
        pos_copy(i).start()
        data_copy(i).start()

    def send_group(k):
        @pl.loop(2 * k, 2 * k + 2)
        def _(pair):
            build(2 * pair)
            build(2 * pair + 1)
            send(2 * pair)
            send(2 * pair + 1)

    def halo_copies():
        found = []
        for side, (start, end, step) in enumerate(((NB, 0, 1), (HALO, LOCAL - HALO, NG - 1))):
            for part, table in enumerate((lx, lw, lq)):
                at = 3 * side + part
                found.append(pltpu.make_async_remote_copy(
                    table.at[pl.ds(start, HALO)], table.at[pl.ds(end, HALO)], s_halo.at[at], r_halo.at[at],
                    device_id=grp_peer(step), device_id_type=MESH))
        return found

    def copy_one(d):
        return pltpu.make_async_remote_copy(
            st1.at[(g + d) % NG], rv1.at[d], s_one.at[d], r_one.at[d], device_id=grp_peer(d), device_id_type=MESH)

    def copy_two(i, sign=1):
        return pltpu.make_async_remote_copy(
            st2.at[row_at(r, i, 1)], rv2.at[i], s_two.at[i], r_two.at[i],
            device_id=row_peer(i, sign), device_id_type=MESH)

    def copy_three(d):
        return pltpu.make_async_remote_copy(
            s2, rv3.at[d], s_three.at[d], r_three.at[d], device_id=grp_peer(d), device_id_type=MESH)

    build(0)
    build(1)
    pl.semaphore_wait(barrier, NR - 1 + (NG - 1 if whole_job else 0))
    send(1)
    inq[0] = outq[0]
    inbox[0] = outbox[0]
    build(2)
    build(3)
    send(2)
    send(3)

    @pl.loop(1, FIRST)
    def _(k):
        send_group(k)

    same = iota((BLK, BLK), 0) == iota((BLK, BLK), 1)
    ones = jnp.ones((BLK, BLK), BF16)
    UNROLL = 4

    @pl.loop(0, NB // UNROLL)
    def _(turn):
        for u in range(UNROLL):
            b = turn * UNROLL + u
            anomaly = anomaly_of(b)
            lx[HALO + b] = anomaly
            place = jnp.broadcast_to(places[b], (BLK, BLK))
            pb[b] = mm(jnp.where(same, place, 0.0).astype(BF16), ones) * ROOT
            acc[b] = jnp.zeros((BLK, MEM), F32)
            if whole_job:
                picks = (iota((BLK, BLK), 0) == obs[b]).astype(BF16)
                seen = (mm(jnp.ones((8, BLK), BF16), picks, NT) > 0.5).astype(BF16)
                summed = mm(picks, wts[b]).astype(BF16)
                lw[HALO + b] = summed
                over[...] += jnp.maximum(mm(seen, ones) - float(sent), 0.0)
                part = mm(summed, anomaly, TN)
                cross_a[...] += part[:, :128]
                cross_b[...] += part[:, 128:]

    if whole_job:
        for d in range(NG):
            st1[d, :, 0:128] = cross_a[pl.ds(d, NR, stride=COLS), :]
            st1[d, :, 128:MEM] = cross_b[pl.ds(d, NR, stride=COLS), :]
            st1[d, :, MEM:WIDE] = jnp.broadcast_to(over[0:1], (NR, WIDE - MEM))

        @pl.loop(1, NG)
        def _(d):
            copy_one(d).start()

        for copy in halo_copies():
            copy.start()

    @pl.loop(FIRST, AHEAD)
    def _(k):
        send_group(k)

    at_block = iota((NB, 128), 0)
    counts = jnp.zeros((NB, 128), jnp.int32)
    for k in range(NB):
        counts = jnp.where(at_block == k, count[k], counts)
    entry = iota((NB, 128), 1)
    found = jnp.zeros((NB, 128), F32)
    for l in range(LISTS):
        hit = (loc[:, l : l + 1] == entry) & (counts > l)
        found = jnp.where(hit, 1.0, found)
    member[...] = found.astype(BF16)

    def masked_place(t, place):
        column = (iota((128, 128), 0) == t).astype(BF16)
        return jnp.where(mm(member[...], column) > 0.5, place * ROOT, FAR)

    def meet(tiles, weights, width, chunk=4):
        for c in range(0, NB, chunk):
            rows = chunk * BLK
            xb = lx[HALO + c : HALO + c + chunk].reshape(rows, MEM)
            score = mm(xb, tiles, NT)
            at_row = jnp.concatenate([pb[c : c + chunk]] * (width // 128), axis=2)
            gap = at_row - qmask[c : c + chunk, :, 0:width]
            den = (gap * gap + (MEM - 1.0)).reshape(rows, width)
            inv = pl.reciprocal(den, approx=True)
            inv = inv * (2.0 - den * inv)
            mix = (score * inv).astype(BF16)
            acc[c : c + chunk] += mm(mix, weights).reshape(chunk, BLK, MEM)

    def put_mask(whole):
        for k in range(NB):
            qmask[k, :, 0 : whole.shape[1]] = whole[k : k + 1]

    if whole_job:

        @pl.loop(0, LOCAL // 2)
        def _(it):
            @pl.when(it == NB // 2)
            def _():
                for copy in halo_copies():
                    copy.wait()

            p = (it + 1) % (LOCAL // 2)
            put_mask(jnp.concatenate([masked_place(2 * p + e, lq[2 * p + e]) for e in range(2)], axis=1))
            tiles = lx[pl.ds(2 * p, 2)].reshape(2 * BLK, MEM)
            weights = lw[pl.ds(2 * p, 2)].reshape(2 * BLK, MEM)
            meet(tiles, weights, 2 * BLK)

    def one_to_two():
        @pl.loop(1, NG)
        def _(d):
            copy_one(d).wait()

        s1 = st1[g]
        for d in range(1, NG):
            s1 = s1 + rv1[d]
        for k in range(NR):
            st2[k] = s1[k : k + 1]

        @pl.loop(1, NR)
        def _(i):
            copy_two(i).start()

        rv2[0] = st2[r]

    def two_to_three():
        @pl.loop(1, NR)
        def _(i):
            copy_two(i, -1).wait()

        total = rv2[0]
        for i in range(1, NR):
            total = total + rv2[i]
        s2[...] = total

        @pl.loop(1, NG)
        def _(d):
            copy_three(d).start()

        rv3[0] = total
        flag_out[...] = total[:, MEM:WIDE]

    def finish_theta():
        @pl.loop(1, NG)
        def _(d):
            copy_three(d).wait()

        found = jnp.zeros((COLS, MEM), F32)
        spot = iota((COLS, MEM), 0)
        for d in range(NG):
            found = jnp.where(spot == (g - d + NG) % NG, rv3[d, :, 0:MEM], found)
        mean = jnp.mean(theta[...], axis=1, keepdims=True)
        update = exact(found, theta[...] - mean, NT)
        chosen = (iota((COLS, MEM), 1) == COLS * r + iota((COLS, MEM), 0)).astype(F32)
        old = exact(chosen, theta[...], NT)
        theta_out[...] = old + update / math.sqrt(MEM * NB * BLK * NG * NR)

    @pl.loop(0, GROUPS)
    def _(it):
        if whole_job:

            @pl.when(it == ONE_AT)
            def _():
                one_to_two()

            @pl.when(it == SUM_AT)
            def _():
                two_to_three()

            @pl.when(it == END_AT)
            def _():
                finish_theta()

        @pl.when(it < GROUPS - AHEAD)
        def _():
            send_group(it + AHEAD)

        for e in range(GROUP):
            i = GROUP * it + e

            @pl.when(i > 0)
            def _():
                pos_copy(i, -1).wait()

        put_mask(side_by_side(
            [masked_place(LOCAL + row_at(r, GROUP * it + e, -1), inq[GROUP * it + e]) for e in range(GROUP)], sent))
        for e in range(GROUP):
            i = GROUP * it + e

            @pl.when(i > 0)
            def _():
                data_copy(i, -1).wait()

        at = pl.ds(GROUP * it, GROUP)
        tiles = inbox[at, 0:sent, :].reshape(GROUP * sent, MEM)
        weights = inbox[at, sent : 2 * sent, :].reshape(GROUP * sent, MEM)
        meet(tiles, weights, GROUP * sent)

    if not whole_job:
        theta_out[...] = jnp.zeros_like(theta_out)
        flag_out[...] = jnp.zeros_like(flag_out)


def analyse(args, first, sent, whole_job):
    vmem, smem = pl.BlockSpec(memory_space=pltpu.VMEM), pl.BlockSpec(memory_space=pltpu.SMEM)
    dma = pltpu.SemaphoreType.DMA
    states, position, obs_row, obs_weight, send_block, loc_table, loc_count, theta = args
    return pl.pallas_call(
        functools.partial(kernel, first, sent, whole_job),
        out_shape=(
            jax.ShapeDtypeStruct((NB, BLK, MEM), F32),
            jax.ShapeDtypeStruct((COLS, PARAMS), F32),
            jax.ShapeDtypeStruct((1, 128), F32),
        ),
        in_specs=[pl.BlockSpec(memory_space=pl.ANY)] * 2 + [vmem] * 4 + [smem] * 2,
        out_specs=(vmem, vmem, vmem),
        scratch_shapes=[
            pltpu.VMEM((NB, BLK, MEM), BF16),
            pltpu.VMEM((NB, BLK, MEM), BF16),
            dma((2,)),
            pltpu.VMEM((NB, 1, BLK), F32),
            pltpu.VMEM((LOCAL, BLK, MEM), BF16),
            pltpu.VMEM((LOCAL, BLK, MEM), BF16),
            pltpu.VMEM((LOCAL, 1, BLK), F32),
            pltpu.VMEM((NR, 2 * sent, MEM), BF16),
            pltpu.VMEM((NR, 1, BLK), F32),
            pltpu.VMEM((NR, 2 * sent, MEM), BF16),
            pltpu.VMEM((NR, 1, BLK), F32),
            pltpu.VMEM((NB, BLK, 128), F32),
            pltpu.VMEM((NB, 128), BF16),
            pltpu.VMEM((NB, 1, GROUP * sent), F32),
            pltpu.VMEM((8, 128), F32),
            pltpu.VMEM((MEM, 128), F32),
            pltpu.VMEM((MEM, 128), F32),
            pltpu.VMEM((NG, NR, WIDE), F32),
            pltpu.VMEM((NG, NR, WIDE), F32),
            pltpu.VMEM((NR, 1, WIDE), F32),
            pltpu.VMEM((NR, 1, WIDE), F32),
            pltpu.VMEM((1, WIDE), F32),
            pltpu.VMEM((NG, 1, WIDE), F32),
            dma((NR,)), dma((NR,)), dma((NR,)), dma((NR,)), dma((6,)), dma((6,)),
            dma((NG,)), dma((NG,)), dma((NR,)), dma((NR,)), dma((NG,)), dma((NG,)),
        ],
        compiler_params=pltpu.CompilerParams(
            collective_id=0 if whole_job else 1, has_side_effects=True, vmem_limit_bytes=48 * 1024 * 1024
        ),
    )(
        states.reshape(NB, BLK, MEM),
        obs_weight.reshape(NB, BLK, MEM),
        position.reshape(NB, BLK),
        obs_row.reshape(NB, 1, BLK),
        loc_table,
        theta,
        send_block.reshape(NR),
        loc_count,
    )


def per_device(*args):
    states = args[0]
    acc, theta_new, flag = analyse(args, 0, SENT, True)

    def add(increment):
        return (states.astype(F32) + increment.reshape(NB * BLK, MEM)).astype(BF16)

    def rest():
        return add(acc + analyse(args, SENT, BLK - SENT, False)[0])

    analysis = add(acc) if SENT == BLK else lax.cond(flag[0, 0] > 0.5, rest, lambda: add(acc))
    return analysis, theta_new.T


def solution(mesh):
    in_specs = (
        P(("grp", "row"), None),
        P(("grp", "row")),
        P(("grp", "row"), None),
        P(("grp", "row"), None),
        P(("grp", "row"), None),
        P(("grp", "row"), None),
        P(("grp", "row")),
        P(),
    )
    out_specs = (P(("grp", "row"), None), P(None, "row"))
    return jax.shard_map(
        per_device, mesh=mesh, in_specs=in_specs, out_specs=out_specs, check_vma=False
    )
```

```python
import functools
import math

import jax
import jax.numpy as jnp
from jax import lax
from jax.experimental import pallas as pl
from jax.experimental.pallas import tpu as pltpu
from jax.sharding import PartitionSpec as P

MESH = pl.DeviceIdType.MESH
NG, NY, NZ = 8, 4, 8
NR = NY * NZ
NB, BLK, MEM = 16, 128, 256
HALO = 2
LOCAL = NB + 2 * HALO
LISTS = 16
PARAMS = 64
COLS = MEM // NR
WIDE = MEM + 128
GROUP = 4
GROUPS = NR // GROUP
FIRST = 2
AHEAD = 4
FLIP = 1
ONE_AT = 1
SUM_AT = 2
END_AT = 6
SENT = 96
ROOT = math.sqrt(MEM - 1.0)
FAR = 1.5e19
F32, BF16 = jnp.float32, jnp.bfloat16
NT = (((1,), (1,)), ((), ()))
TN = (((0,), (0,)), ((), ()))


def mm(a, b, dims=(((1,), (0,)), ((), ()))):
    return lax.dot_general(a, b, dims, preferred_element_type=F32)


def exact(a, b, dims):
    return lax.dot_general(a, b, dims, precision=lax.Precision.HIGHEST, preferred_element_type=F32)


def iota(shape, dim):
    return lax.broadcasted_iota(jnp.int32, shape, dim)


def row_at(r, i, sign):
    div, rem = (int.__floordiv__, int.__mod__) if isinstance(i, int) else (lax.div, lax.rem)
    part, dy, side = div(i, 2 * NY), rem(div(i, 2), NY), rem(i, 2)
    far = div(part + 3, 4)
    hops = far * (FLIP * (4 - 2 * part) + part)
    dz = side * (NZ - hops - (1 - far) * (NZ // 2)) + (1 - side) * hops
    y, z = lax.div(r, NZ), lax.rem(r, NZ)
    return lax.rem(y + sign * dy + NY, NY) * NZ + lax.rem(z + sign * dz + NZ, NZ)


def side_by_side(parts, width):
    if width == 128:
        return jnp.concatenate(parts, axis=1)
    lane = iota(parts[0].shape, 1)
    a, b, c, d = parts
    if width == 96:
        b, c, d = pltpu.roll(b, 96, 1), pltpu.roll(c, 64, 1), pltpu.roll(d, 32, 1)
        return jnp.concatenate(
            [jnp.where(lane < 96, a, b), jnp.where(lane < 64, b, c), jnp.where(lane < 32, c, d)], axis=1)
    assert width == 32
    b, c, d = pltpu.roll(b, 32, 1), pltpu.roll(c, 64, 1), pltpu.roll(d, 96, 1)
    return jnp.where(lane < 32, a, jnp.where(lane < 64, b, jnp.where(lane < 96, c, d)))


def observed_rows(obs_row):
    picks = (iota((BLK, BLK), 0) == obs_row).astype(BF16)
    below = (iota((BLK, BLK), 0) < iota((BLK, BLK), 1)).astype(BF16)
    seen = (mm(jnp.ones((8, BLK), BF16), picks, NT) > 0.5).astype(BF16)
    rank = mm(seen, below)
    at = iota((BLK, BLK), 0).astype(F32)
    pack = jnp.where(at == rank[0:1], seen[0:1].astype(F32), 0.0).astype(BF16)
    return picks, seen, pack


def kernel(
    first, sent, whole_job,
    states_in, wts_in, pos, obs, loc, theta, send_block, count, acc, theta_out, flag_out,
    states, wts, load, places, lx, lw, lq, outbox, outq, inbox, inq, pb, member, qmask, over,
    cross_a, cross_b, st1, rv1, st2, rv2, s2, rv3,
    s_data, r_data, s_pos, r_pos, s_halo, r_halo, s_one, r_one, s_two, r_two, s_three, r_three, row_in, grp_in,
):
    g, r = lax.axis_index("grp"), lax.axis_index("row")

    def row_peer(i, sign=1):
        return (g, row_at(r, i, sign))

    def grp_peer(d):
        return ((g + d) % NG, r)

    barrier = pltpu.get_barrier_semaphore()

    loads = [
        pltpu.make_async_copy(states_in, states, load.at[0]), pltpu.make_async_copy(wts_in, wts, load.at[1])]
    for copy in loads:
        copy.start()
    y, z = lax.div(r, NZ), lax.rem(r, NZ)
    y_line = [(g, lax.rem(y + d, NY) * NZ + z) for d in range(1, NY)]
    z_line = [(g, y * NZ + lax.rem(z + d, NZ)) for d in (4, 3, 5, 2, 6, 1, 7)]
    other_core = (g + 1 - 2 * lax.rem(g, 2), r)
    x_line = [(lax.rem(g + d, NG), r) for d in range(2, NG, 2)]
    greeted = z_line + y_line + ([other_core] + x_line if whole_job else [])
    for peer in greeted:
        pl.semaphore_signal(barrier, inc=1, device_id=peer, device_id_type=MESH)
    if whole_job:
        cross_a[...] = jnp.zeros_like(cross_a)
        cross_b[...] = jnp.zeros_like(cross_b)
        over[...] = jnp.zeros_like(over)

    for b in range(NB):
        place = pos[b : b + 1].astype(F32)
        places[b] = place
        lq[HALO + b] = place

    for copy in loads:
        copy.wait()

    def data_copy(i, sign=1):
        return pltpu.make_async_remote_copy(
            outbox.at[i], inbox.at[i], s_data.at[i], r_data.at[i],
            device_id=row_peer(i, sign), device_id_type=MESH)

    def pos_copy(i, sign=1):
        return pltpu.make_async_remote_copy(
            outq.at[i], inq.at[i], s_pos.at[i], r_pos.at[i],
            device_id=row_peer(i, sign), device_id_type=MESH)

    def anomaly_of(b):
        whole = states[b].astype(F32)
        return (whole - jnp.mean(whole, axis=1, keepdims=True)).astype(BF16)

    def build(i):
        b = send_block[row_at(r, i, 1)]
        anomaly, weights = anomaly_of(b), wts[b]
        picks, _, pack = observed_rows(obs[b])
        summed = mm(picks, weights).astype(BF16)
        outbox[i, 0:sent] = mm(pack, anomaly).astype(BF16)[first : first + sent]
        outbox[i, sent : 2 * sent] = mm(pack, summed).astype(BF16)[first : first + sent]
        place = jnp.broadcast_to(places[b], (16, BLK)).astype(BF16)
        packed = mm(place, pack, NT)[0:1]
        outq[i] = packed if first == 0 else pltpu.roll(packed, BLK - first, 1)

    def send(i):
        pos_copy(i).start()
        data_copy(i).start()

    def send_group(k):
        @pl.loop(2 * k, 2 * k + 2)
        def _(pair):
            build(2 * pair)
            build(2 * pair + 1)
            send(2 * pair)
            send(2 * pair + 1)

    def halo_copies():
        found = []
        for side, (start, end, step) in enumerate(((NB, 0, 1), (HALO, LOCAL - HALO, NG - 1))):
            for part, table in enumerate((lx, lw, lq)):
                at = 3 * side + part
                found.append(pltpu.make_async_remote_copy(
                    table.at[pl.ds(start, HALO)], table.at[pl.ds(end, HALO)], s_halo.at[at], r_halo.at[at],
                    device_id=grp_peer(step), device_id_type=MESH))
        return found

    def copy_one(d):
        return pltpu.make_async_remote_copy(
            st1.at[(g + d) % NG], rv1.at[d], s_one.at[d], r_one.at[d], device_id=grp_peer(d), device_id_type=MESH)

    def copy_two(i, sign=1):
        return pltpu.make_async_remote_copy(
            st2.at[row_at(r, i, 1)], rv2.at[i], s_two.at[i], r_two.at[i],
            device_id=row_peer(i, sign), device_id_type=MESH)

    def copy_three(d):
        return pltpu.make_async_remote_copy(
            s2, rv3.at[d], s_three.at[d], r_three.at[d], device_id=grp_peer(d), device_id_type=MESH)

    build(0)
    build(1)
    pl.semaphore_wait(barrier, len(greeted))
    for peer in y_line:
        pl.semaphore_signal(row_in, inc=1, device_id=peer, device_id_type=MESH)
    if whole_job:
        pl.semaphore_signal(grp_in, inc=1, device_id=other_core, device_id_type=MESH)
    send(1)
    inq[0] = outq[0]
    inbox[0] = outbox[0]
    build(2)
    build(3)
    pl.semaphore_wait(row_in, NY - 1)
    if whole_job:
        pl.semaphore_wait(grp_in, 1)
    send(2)
    send(3)

    @pl.loop(1, FIRST)
    def _(k):
        send_group(k)

    same = iota((BLK, BLK), 0) == iota((BLK, BLK), 1)
    ones = jnp.ones((BLK, BLK), BF16)
    UNROLL = 4

    @pl.loop(0, NB // UNROLL)
    def _(turn):
        for u in range(UNROLL):
            b = turn * UNROLL + u
            anomaly = anomaly_of(b)
            lx[HALO + b] = anomaly
            place = jnp.broadcast_to(places[b], (BLK, BLK))
            pb[b] = mm(jnp.where(same, place, 0.0).astype(BF16), ones) * ROOT
            acc[b] = jnp.zeros((BLK, MEM), F32)
            if whole_job:
                picks = (iota((BLK, BLK), 0) == obs[b]).astype(BF16)
                seen = (mm(jnp.ones((8, BLK), BF16), picks, NT) > 0.5).astype(BF16)
                summed = mm(picks, wts[b]).astype(BF16)
                lw[HALO + b] = summed
                over[...] += jnp.maximum(mm(seen, ones) - float(sent), 0.0)
                part = mm(summed, anomaly, TN)
                cross_a[...] += part[:, :128]
                cross_b[...] += part[:, 128:]

    if whole_job:
        for d in range(NG):
            st1[d, :, 0:128] = cross_a[pl.ds(d, NR, stride=COLS), :]
            st1[d, :, 128:MEM] = cross_b[pl.ds(d, NR, stride=COLS), :]
            st1[d, :, MEM:WIDE] = jnp.broadcast_to(over[0:1], (NR, WIDE - MEM))

        @pl.loop(1, NG)
        def _(d):
            copy_one(d).start()

        for copy in halo_copies():
            copy.start()

    @pl.loop(FIRST, AHEAD)
    def _(k):
        send_group(k)

    at_block = iota((NB, 128), 0)
    counts = jnp.zeros((NB, 128), jnp.int32)
    for k in range(NB):
        counts = jnp.where(at_block == k, count[k], counts)
    entry = iota((NB, 128), 1)
    found = jnp.zeros((NB, 128), F32)
    for l in range(LISTS):
        hit = (loc[:, l : l + 1] == entry) & (counts > l)
        found = jnp.where(hit, 1.0, found)
    member[...] = found.astype(BF16)

    def masked_place(t, place):
        column = (iota((128, 128), 0) == t).astype(BF16)
        return jnp.where(mm(member[...], column) > 0.5, place * ROOT, FAR)

    def meet(tiles, weights, width, chunk=4):
        for c in range(0, NB, chunk):
            rows = chunk * BLK
            xb = lx[HALO + c : HALO + c + chunk].reshape(rows, MEM)
            score = mm(xb, tiles, NT)
            at_row = jnp.concatenate([pb[c : c + chunk]] * (width // 128), axis=2)
            gap = at_row - qmask[c : c + chunk, :, 0:width]
            den = (gap * gap + (MEM - 1.0)).reshape(rows, width)
            inv = pl.reciprocal(den, approx=True)
            inv = inv * (2.0 - den * inv)
            mix = (score * inv).astype(BF16)
            acc[c : c + chunk] += mm(mix, weights).reshape(chunk, BLK, MEM)

    def put_mask(whole):
        for k in range(NB):
            qmask[k, :, 0 : whole.shape[1]] = whole[k : k + 1]

    if whole_job:

        @pl.loop(0, LOCAL // 2)
        def _(it):
            @pl.when(it == NB // 2)
            def _():
                for copy in halo_copies():
                    copy.wait()

            p = (it + 1) % (LOCAL // 2)
            put_mask(jnp.concatenate([masked_place(2 * p + e, lq[2 * p + e]) for e in range(2)], axis=1))
            tiles = lx[pl.ds(2 * p, 2)].reshape(2 * BLK, MEM)
            weights = lw[pl.ds(2 * p, 2)].reshape(2 * BLK, MEM)
            meet(tiles, weights, 2 * BLK)

    def one_to_two():
        @pl.loop(1, NG)
        def _(d):
            copy_one(d).wait()

        s1 = st1[g]
        for d in range(1, NG):
            s1 = s1 + rv1[d]
        for k in range(NR):
            st2[k] = s1[k : k + 1]

        @pl.loop(1, NR)
        def _(i):
            copy_two(i).start()

        rv2[0] = st2[r]

    def two_to_three():
        @pl.loop(1, NR)
        def _(i):
            copy_two(i, -1).wait()

        total = rv2[0]
        for i in range(1, NR):
            total = total + rv2[i]
        s2[...] = total

        @pl.loop(1, NG)
        def _(d):
            copy_three(d).start()

        rv3[0] = total
        flag_out[...] = total[:, MEM:WIDE]

    def finish_theta():
        @pl.loop(1, NG)
        def _(d):
            copy_three(d).wait()

        found = jnp.zeros((COLS, MEM), F32)
        spot = iota((COLS, MEM), 0)
        for d in range(NG):
            found = jnp.where(spot == (g - d + NG) % NG, rv3[d, :, 0:MEM], found)
        mean = jnp.mean(theta[...], axis=1, keepdims=True)
        update = exact(found, theta[...] - mean, NT)
        chosen = (iota((COLS, MEM), 1) == COLS * r + iota((COLS, MEM), 0)).astype(F32)
        old = exact(chosen, theta[...], NT)
        theta_out[...] = old + update / math.sqrt(MEM * NB * BLK * NG * NR)

    @pl.loop(0, GROUPS)
    def _(it):
        if whole_job:

            @pl.when(it == ONE_AT)
            def _():
                one_to_two()

            @pl.when(it == SUM_AT)
            def _():
                two_to_three()

            @pl.when(it == END_AT)
            def _():
                finish_theta()

        @pl.when(it < GROUPS - AHEAD)
        def _():
            send_group(it + AHEAD)

        for e in range(GROUP):
            i = GROUP * it + e

            @pl.when(i > 0)
            def _():
                pos_copy(i, -1).wait()

        put_mask(side_by_side(
            [masked_place(LOCAL + row_at(r, GROUP * it + e, -1), inq[GROUP * it + e]) for e in range(GROUP)], sent))
        for e in range(GROUP):
            i = GROUP * it + e

            @pl.when(i > 0)
            def _():
                data_copy(i, -1).wait()

        at = pl.ds(GROUP * it, GROUP)
        tiles = inbox[at, 0:sent, :].reshape(GROUP * sent, MEM)
        weights = inbox[at, sent : 2 * sent, :].reshape(GROUP * sent, MEM)
        meet(tiles, weights, GROUP * sent)

    if not whole_job:
        theta_out[...] = jnp.zeros_like(theta_out)
        flag_out[...] = jnp.zeros_like(flag_out)


def analyse(args, first, sent, whole_job):
    vmem, smem = pl.BlockSpec(memory_space=pltpu.VMEM), pl.BlockSpec(memory_space=pltpu.SMEM)
    dma = pltpu.SemaphoreType.DMA
    states, position, obs_row, obs_weight, send_block, loc_table, loc_count, theta = args
    return pl.pallas_call(
        functools.partial(kernel, first, sent, whole_job),
        out_shape=(
            jax.ShapeDtypeStruct((NB, BLK, MEM), F32),
            jax.ShapeDtypeStruct((COLS, PARAMS), F32),
            jax.ShapeDtypeStruct((1, 128), F32),
        ),
        in_specs=[pl.BlockSpec(memory_space=pl.ANY)] * 2 + [vmem] * 4 + [smem] * 2,
        out_specs=(vmem, vmem, vmem),
        scratch_shapes=[
            pltpu.VMEM((NB, BLK, MEM), BF16),
            pltpu.VMEM((NB, BLK, MEM), BF16),
            dma((2,)),
            pltpu.VMEM((NB, 1, BLK), F32),
            pltpu.VMEM((LOCAL, BLK, MEM), BF16),
            pltpu.VMEM((LOCAL, BLK, MEM), BF16),
            pltpu.VMEM((LOCAL, 1, BLK), F32),
            pltpu.VMEM((NR, 2 * sent, MEM), BF16),
            pltpu.VMEM((NR, 1, BLK), F32),
            pltpu.VMEM((NR, 2 * sent, MEM), BF16),
            pltpu.VMEM((NR, 1, BLK), F32),
            pltpu.VMEM((NB, BLK, 128), F32),
            pltpu.VMEM((NB, 128), BF16),
            pltpu.VMEM((NB, 1, GROUP * sent), F32),
            pltpu.VMEM((8, 128), F32),
            pltpu.VMEM((MEM, 128), F32),
            pltpu.VMEM((MEM, 128), F32),
            pltpu.VMEM((NG, NR, WIDE), F32),
            pltpu.VMEM((NG, NR, WIDE), F32),
            pltpu.VMEM((NR, 1, WIDE), F32),
            pltpu.VMEM((NR, 1, WIDE), F32),
            pltpu.VMEM((1, WIDE), F32),
            pltpu.VMEM((NG, 1, WIDE), F32),
            dma((NR,)), dma((NR,)), dma((NR,)), dma((NR,)), dma((6,)), dma((6,)),
            dma((NG,)), dma((NG,)), dma((NR,)), dma((NR,)), dma((NG,)), dma((NG,)),
            pltpu.SemaphoreType.REGULAR, pltpu.SemaphoreType.REGULAR,
        ],
        compiler_params=pltpu.CompilerParams(
            collective_id=0 if whole_job else 1, has_side_effects=True, vmem_limit_bytes=48 * 1024 * 1024
        ),
    )(
        states.reshape(NB, BLK, MEM),
        obs_weight.reshape(NB, BLK, MEM),
        position.reshape(NB, BLK),
        obs_row.reshape(NB, 1, BLK),
        loc_table,
        theta,
        send_block.reshape(NR),
        loc_count,
    )


def per_device(*args):
    states = args[0]
    acc, theta_new, flag = analyse(args, 0, SENT, True)

    def add(increment):
        return (states.astype(F32) + increment.reshape(NB * BLK, MEM)).astype(BF16)

    def rest():
        return add(acc + analyse(args, SENT, BLK - SENT, False)[0])

    analysis = add(acc) if SENT == BLK else lax.cond(flag[0, 0] > 0.5, rest, lambda: add(acc))
    return analysis, theta_new.T


def solution(mesh):
    in_specs = (
        P(("grp", "row"), None),
        P(("grp", "row")),
        P(("grp", "row"), None),
        P(("grp", "row"), None),
        P(("grp", "row"), None),
        P(("grp", "row"), None),
        P(("grp", "row")),
        P(),
    )
    out_specs = (P(("grp", "row"), None), P(None, "row"))
    return jax.shard_map(
        per_device, mesh=mesh, in_specs=in_specs, out_specs=out_specs, check_vma=False
    )
```

```python
import functools
import math

import jax
import jax.numpy as jnp
from jax import lax
from jax.experimental import pallas as pl
from jax.experimental.pallas import tpu as pltpu
from jax.sharding import PartitionSpec as P

MESH = pl.DeviceIdType.MESH
NG, NY, NZ = 8, 4, 8
NR = NY * NZ
NB, BLK, MEM = 16, 128, 256
HALO = 2
LOCAL = NB + 2 * HALO
LISTS = 16
PARAMS = 64
COLS = MEM // NR
WIDE = MEM + 128
GROUP = 4
GROUPS = NR // GROUP
FIRST = 2
AHEAD = 4
FLIP = 1
ONE_AT = 1
SUM_AT = 3
END_AT = 6
SENT = 96
ROOT = math.sqrt(MEM - 1.0)
FAR = 1.5e19
F32, BF16 = jnp.float32, jnp.bfloat16
NT = (((1,), (1,)), ((), ()))
TN = (((0,), (0,)), ((), ()))


def mm(a, b, dims=(((1,), (0,)), ((), ()))):
    return lax.dot_general(a, b, dims, preferred_element_type=F32)


def exact(a, b, dims):
    return lax.dot_general(a, b, dims, precision=lax.Precision.HIGHEST, preferred_element_type=F32)


def iota(shape, dim):
    return lax.broadcasted_iota(jnp.int32, shape, dim)


def row_at(r, i, sign):
    div, rem = (int.__floordiv__, int.__mod__) if isinstance(i, int) else (lax.div, lax.rem)
    part, dy, side = div(i, 2 * NY), rem(div(i, 2), NY), rem(i, 2)
    far = div(part + 3, 4)
    hops = far * (FLIP * (4 - 2 * part) + part)
    dz = side * (NZ - hops - (1 - far) * (NZ // 2)) + (1 - side) * hops
    y, z = lax.div(r, NZ), lax.rem(r, NZ)
    return lax.rem(y + sign * dy + NY, NY) * NZ + lax.rem(z + sign * dz + NZ, NZ)


def side_by_side(parts, width):
    if width == 128:
        return jnp.concatenate(parts, axis=1)
    lane = iota(parts[0].shape, 1)
    a, b, c, d = parts
    if width == 96:
        b, c, d = pltpu.roll(b, 96, 1), pltpu.roll(c, 64, 1), pltpu.roll(d, 32, 1)
        return jnp.concatenate(
            [jnp.where(lane < 96, a, b), jnp.where(lane < 64, b, c), jnp.where(lane < 32, c, d)], axis=1)
    assert width == 32
    b, c, d = pltpu.roll(b, 32, 1), pltpu.roll(c, 64, 1), pltpu.roll(d, 96, 1)
    return jnp.where(lane < 32, a, jnp.where(lane < 64, b, jnp.where(lane < 96, c, d)))


def observed_rows(obs_row):
    picks = (iota((BLK, BLK), 0) == obs_row).astype(BF16)
    below = (iota((BLK, BLK), 0) < iota((BLK, BLK), 1)).astype(BF16)
    seen = (mm(jnp.ones((8, BLK), BF16), picks, NT) > 0.5).astype(BF16)
    rank = mm(seen, below)
    at = iota((BLK, BLK), 0).astype(F32)
    pack = jnp.where(at == rank[0:1], seen[0:1].astype(F32), 0.0).astype(BF16)
    return picks, seen, pack


def kernel(
    first, sent, whole_job,
    states_in, wts_in, pos, obs, loc, theta, send_block, count, acc, theta_out, flag_out,
    states, wts, load, places, lx, lw, lq, outbox, outq, inbox, inq, pb, member, qmask, over,
    cross_a, cross_b, st1, rv1, st2, rv2, s2, rv3,
    s_data, r_data, s_pos, r_pos, s_halo, r_halo, s_one, r_one, s_two, r_two, s_three, r_three, row_in, grp_in,
):
    g, r = lax.axis_index("grp"), lax.axis_index("row")

    def row_peer(i, sign=1):
        return (g, row_at(r, i, sign))

    def grp_peer(d):
        return ((g + d) % NG, r)

    barrier = pltpu.get_barrier_semaphore()

    loads = [
        pltpu.make_async_copy(states_in, states, load.at[0]), pltpu.make_async_copy(wts_in, wts, load.at[1])]
    for copy in loads:
        copy.start()
    y, z = lax.div(r, NZ), lax.rem(r, NZ)
    y_line = [(g, lax.rem(y + d, NY) * NZ + z) for d in range(1, NY)]
    z_line = [(g, y * NZ + lax.rem(z + d, NZ)) for d in (4, 3, 5, 2, 6, 1, 7)]
    other_core = (g + 1 - 2 * lax.rem(g, 2), r)
    x_line = [(lax.rem(g + d, NG), r) for d in range(2, NG, 2)]
    greeted = z_line + y_line + ([other_core] + x_line if whole_job else [])
    for peer in greeted:
        pl.semaphore_signal(barrier, inc=1, device_id=peer, device_id_type=MESH)
    if whole_job:
        cross_a[...] = jnp.zeros_like(cross_a)
        cross_b[...] = jnp.zeros_like(cross_b)
        over[...] = jnp.zeros_like(over)

    for b in range(NB):
        place = pos[b : b + 1].astype(F32)
        places[b] = place
        lq[HALO + b] = place

    for copy in loads:
        copy.wait()

    def data_copy(i, sign=1):
        return pltpu.make_async_remote_copy(
            outbox.at[i], inbox.at[i], s_data.at[i], r_data.at[i],
            device_id=row_peer(i, sign), device_id_type=MESH)

    def pos_copy(i, sign=1):
        return pltpu.make_async_remote_copy(
            outq.at[i], inq.at[i], s_pos.at[i], r_pos.at[i],
            device_id=row_peer(i, sign), device_id_type=MESH)

    def anomaly_of(b):
        whole = states[b].astype(F32)
        return (whole - jnp.mean(whole, axis=1, keepdims=True)).astype(BF16)

    def build(i):
        b = send_block[row_at(r, i, 1)]
        anomaly, weights = anomaly_of(b), wts[b]
        picks, _, pack = observed_rows(obs[b])
        summed = mm(picks, weights).astype(BF16)
        outbox[i, 0:sent] = mm(pack, anomaly).astype(BF16)[first : first + sent]
        outbox[i, sent : 2 * sent] = mm(pack, summed).astype(BF16)[first : first + sent]
        place = jnp.broadcast_to(places[b], (16, BLK)).astype(BF16)
        packed = mm(place, pack, NT)[0:1]
        outq[i] = packed if first == 0 else pltpu.roll(packed, BLK - first, 1)

    def send(i):
        pos_copy(i).start()
        data_copy(i).start()

    def send_group(k):
        @pl.loop(2 * k, 2 * k + 2)
        def _(pair):
            build(2 * pair)
            build(2 * pair + 1)
            send(2 * pair)
            send(2 * pair + 1)

    def halo_copies():
        found = []
        for side, (start, end, step) in enumerate(((NB, 0, 1), (HALO, LOCAL - HALO, NG - 1))):
            for part, table in enumerate((lx, lw, lq)):
                at = 3 * side + part
                found.append(pltpu.make_async_remote_copy(
                    table.at[pl.ds(start, HALO)], table.at[pl.ds(end, HALO)], s_halo.at[at], r_halo.at[at],
                    device_id=grp_peer(step), device_id_type=MESH))
        return found

    def copy_one(d):
        return pltpu.make_async_remote_copy(
            st1.at[(g + d) % NG], rv1.at[d], s_one.at[d], r_one.at[d], device_id=grp_peer(d), device_id_type=MESH)

    def copy_two(i, sign=1):
        return pltpu.make_async_remote_copy(
            st2.at[row_at(r, i, 1)], rv2.at[i], s_two.at[i], r_two.at[i],
            device_id=row_peer(i, sign), device_id_type=MESH)

    def copy_three(d):
        return pltpu.make_async_remote_copy(
            s2, rv3.at[d], s_three.at[d], r_three.at[d], device_id=grp_peer(d), device_id_type=MESH)

    build(0)
    build(1)
    pl.semaphore_wait(barrier, len(greeted))
    for peer in y_line:
        pl.semaphore_signal(row_in, inc=1, device_id=peer, device_id_type=MESH)
    if whole_job:
        pl.semaphore_signal(grp_in, inc=1, device_id=other_core, device_id_type=MESH)
    send(1)
    inq[0] = outq[0]
    inbox[0] = outbox[0]
    build(2)
    build(3)
    pl.semaphore_wait(row_in, NY - 1)
    if whole_job:
        pl.semaphore_wait(grp_in, 1)
    send(2)
    send(3)

    @pl.loop(1, FIRST)
    def _(k):
        send_group(k)

    same = iota((BLK, BLK), 0) == iota((BLK, BLK), 1)
    ones = jnp.ones((BLK, BLK), BF16)
    UNROLL = 4

    @pl.loop(0, NB // UNROLL)
    def _(turn):
        for u in range(UNROLL):
            b = turn * UNROLL + u
            anomaly = anomaly_of(b)
            lx[HALO + b] = anomaly
            place = jnp.broadcast_to(places[b], (BLK, BLK))
            pb[b] = mm(jnp.where(same, place, 0.0).astype(BF16), ones) * ROOT
            acc[b] = jnp.zeros((BLK, MEM), F32)
            if whole_job:
                picks = (iota((BLK, BLK), 0) == obs[b]).astype(BF16)
                seen = (mm(jnp.ones((8, BLK), BF16), picks, NT) > 0.5).astype(BF16)
                summed = mm(picks, wts[b]).astype(BF16)
                lw[HALO + b] = summed
                over[...] += jnp.maximum(mm(seen, ones) - float(sent), 0.0)
                part = mm(summed, anomaly, TN)
                cross_a[...] += part[:, :128]
                cross_b[...] += part[:, 128:]

    if whole_job:
        for d in range(NG):
            st1[d, :, 0:128] = cross_a[pl.ds(d, NR, stride=COLS), :]
            st1[d, :, 128:MEM] = cross_b[pl.ds(d, NR, stride=COLS), :]
            st1[d, :, MEM:WIDE] = jnp.broadcast_to(over[0:1], (NR, WIDE - MEM))

        @pl.loop(1, NG)
        def _(d):
            copy_one(d).start()

        for copy in halo_copies():
            copy.start()

    @pl.loop(FIRST, AHEAD)
    def _(k):
        send_group(k)

    at_block = iota((NB, 128), 0)
    counts = jnp.zeros((NB, 128), jnp.int32)
    for k in range(NB):
        counts = jnp.where(at_block == k, count[k], counts)
    entry = iota((NB, 128), 1)
    found = jnp.zeros((NB, 128), F32)
    for l in range(LISTS):
        hit = (loc[:, l : l + 1] == entry) & (counts > l)
        found = jnp.where(hit, 1.0, found)
    member[...] = found.astype(BF16)

    def masked_place(t, place):
        column = (iota((128, 128), 0) == t).astype(BF16)
        return jnp.where(mm(member[...], column) > 0.5, place * ROOT, FAR)

    def meet(tiles, weights, width, chunk=4):
        for c in range(0, NB, chunk):
            rows = chunk * BLK
            xb = lx[HALO + c : HALO + c + chunk].reshape(rows, MEM)
            score = mm(xb, tiles, NT)
            at_row = jnp.concatenate([pb[c : c + chunk]] * (width // 128), axis=2)
            gap = at_row - qmask[c : c + chunk, :, 0:width]
            den = (gap * gap + (MEM - 1.0)).reshape(rows, width)
            inv = pl.reciprocal(den, approx=True)
            inv = inv * (2.0 - den * inv)
            mix = (score * inv).astype(BF16)
            acc[c : c + chunk] += mm(mix, weights).reshape(chunk, BLK, MEM)

    def put_mask(whole):
        for k in range(NB):
            qmask[k, :, 0 : whole.shape[1]] = whole[k : k + 1]

    if whole_job:

        @pl.loop(0, LOCAL // 2)
        def _(it):
            @pl.when(it == NB // 2)
            def _():
                for copy in halo_copies():
                    copy.wait()

            p = (it + 1) % (LOCAL // 2)
            put_mask(jnp.concatenate([masked_place(2 * p + e, lq[2 * p + e]) for e in range(2)], axis=1))
            tiles = lx[pl.ds(2 * p, 2)].reshape(2 * BLK, MEM)
            weights = lw[pl.ds(2 * p, 2)].reshape(2 * BLK, MEM)
            meet(tiles, weights, 2 * BLK)

    def one_to_two():
        @pl.loop(1, NG)
        def _(d):
            copy_one(d).wait()

        s1 = st1[g]
        for d in range(1, NG):
            s1 = s1 + rv1[d]
        for k in range(NR):
            st2[k] = s1[k : k + 1]

        @pl.loop(1, NR)
        def _(i):
            copy_two(i).start()

        rv2[0] = st2[r]

    def two_to_three():
        @pl.loop(1, NR)
        def _(i):
            copy_two(i, -1).wait()

        total = rv2[0]
        for i in range(1, NR):
            total = total + rv2[i]
        s2[...] = total

        @pl.loop(1, NG)
        def _(d):
            copy_three(d).start()

        rv3[0] = total
        flag_out[...] = total[:, MEM:WIDE]

    def finish_theta():
        @pl.loop(1, NG)
        def _(d):
            copy_three(d).wait()

        found = jnp.zeros((COLS, MEM), F32)
        spot = iota((COLS, MEM), 0)
        for d in range(NG):
            found = jnp.where(spot == (g - d + NG) % NG, rv3[d, :, 0:MEM], found)
        mean = jnp.mean(theta[...], axis=1, keepdims=True)
        update = exact(found, theta[...] - mean, NT)
        chosen = (iota((COLS, MEM), 1) == COLS * r + iota((COLS, MEM), 0)).astype(F32)
        old = exact(chosen, theta[...], NT)
        theta_out[...] = old + update / math.sqrt(MEM * NB * BLK * NG * NR)

    @pl.loop(0, GROUPS)
    def _(it):
        if whole_job:

            @pl.when(it == ONE_AT)
            def _():
                one_to_two()

            @pl.when(it == SUM_AT)
            def _():
                two_to_three()

            @pl.when(it == END_AT)
            def _():
                finish_theta()

        @pl.when(it < GROUPS - AHEAD)
        def _():
            send_group(it + AHEAD)

        for e in range(GROUP):
            i = GROUP * it + e

            @pl.when(i > 0)
            def _():
                pos_copy(i, -1).wait()

        put_mask(side_by_side(
            [masked_place(LOCAL + row_at(r, GROUP * it + e, -1), inq[GROUP * it + e]) for e in range(GROUP)], sent))
        for e in range(GROUP):
            i = GROUP * it + e

            @pl.when(i > 0)
            def _():
                data_copy(i, -1).wait()

        at = pl.ds(GROUP * it, GROUP)
        tiles = inbox[at, 0:sent, :].reshape(GROUP * sent, MEM)
        weights = inbox[at, sent : 2 * sent, :].reshape(GROUP * sent, MEM)
        meet(tiles, weights, GROUP * sent)

    if not whole_job:
        theta_out[...] = jnp.zeros_like(theta_out)
        flag_out[...] = jnp.zeros_like(flag_out)


def analyse(args, first, sent, whole_job):
    vmem, smem = pl.BlockSpec(memory_space=pltpu.VMEM), pl.BlockSpec(memory_space=pltpu.SMEM)
    dma = pltpu.SemaphoreType.DMA
    states, position, obs_row, obs_weight, send_block, loc_table, loc_count, theta = args
    return pl.pallas_call(
        functools.partial(kernel, first, sent, whole_job),
        out_shape=(
            jax.ShapeDtypeStruct((NB, BLK, MEM), F32),
            jax.ShapeDtypeStruct((COLS, PARAMS), F32),
            jax.ShapeDtypeStruct((1, 128), F32),
        ),
        in_specs=[pl.BlockSpec(memory_space=pl.ANY)] * 2 + [vmem] * 4 + [smem] * 2,
        out_specs=(vmem, vmem, vmem),
        scratch_shapes=[
            pltpu.VMEM((NB, BLK, MEM), BF16),
            pltpu.VMEM((NB, BLK, MEM), BF16),
            dma((2,)),
            pltpu.VMEM((NB, 1, BLK), F32),
            pltpu.VMEM((LOCAL, BLK, MEM), BF16),
            pltpu.VMEM((LOCAL, BLK, MEM), BF16),
            pltpu.VMEM((LOCAL, 1, BLK), F32),
            pltpu.VMEM((NR, 2 * sent, MEM), BF16),
            pltpu.VMEM((NR, 1, BLK), F32),
            pltpu.VMEM((NR, 2 * sent, MEM), BF16),
            pltpu.VMEM((NR, 1, BLK), F32),
            pltpu.VMEM((NB, BLK, 128), F32),
            pltpu.VMEM((NB, 128), BF16),
            pltpu.VMEM((NB, 1, GROUP * sent), F32),
            pltpu.VMEM((8, 128), F32),
            pltpu.VMEM((MEM, 128), F32),
            pltpu.VMEM((MEM, 128), F32),
            pltpu.VMEM((NG, NR, WIDE), F32),
            pltpu.VMEM((NG, NR, WIDE), F32),
            pltpu.VMEM((NR, 1, WIDE), F32),
            pltpu.VMEM((NR, 1, WIDE), F32),
            pltpu.VMEM((1, WIDE), F32),
            pltpu.VMEM((NG, 1, WIDE), F32),
            dma((NR,)), dma((NR,)), dma((NR,)), dma((NR,)), dma((6,)), dma((6,)),
            dma((NG,)), dma((NG,)), dma((NR,)), dma((NR,)), dma((NG,)), dma((NG,)),
            pltpu.SemaphoreType.REGULAR, pltpu.SemaphoreType.REGULAR,
        ],
        compiler_params=pltpu.CompilerParams(
            collective_id=0 if whole_job else 1, has_side_effects=True, vmem_limit_bytes=48 * 1024 * 1024
        ),
    )(
        states.reshape(NB, BLK, MEM),
        obs_weight.reshape(NB, BLK, MEM),
        position.reshape(NB, BLK),
        obs_row.reshape(NB, 1, BLK),
        loc_table,
        theta,
        send_block.reshape(NR),
        loc_count,
    )


def per_device(*args):
    states = args[0]
    acc, theta_new, flag = analyse(args, 0, SENT, True)

    def add(increment):
        return (states.astype(F32) + increment.reshape(NB * BLK, MEM)).astype(BF16)

    def rest():
        return add(acc + analyse(args, SENT, BLK - SENT, False)[0])

    analysis = add(acc) if SENT == BLK else lax.cond(flag[0, 0] > 0.5, rest, lambda: add(acc))
    return analysis, theta_new.T


def solution(mesh):
    in_specs = (
        P(("grp", "row"), None),
        P(("grp", "row")),
        P(("grp", "row"), None),
        P(("grp", "row"), None),
        P(("grp", "row"), None),
        P(("grp", "row"), None),
        P(("grp", "row")),
        P(),
    )
    out_specs = (P(("grp", "row"), None), P(None, "row"))
    return jax.shard_map(
        per_device, mesh=mesh, in_specs=in_specs, out_specs=out_specs, check_vma=False
    )
```
